32 devices in a mesh: groups: 2 (over y), tensor: 4 (over z), dp: 2 (over x), pipe: 2 (over core).
Axes of the slice: x: 2, y: 2, z: 4, core: 2. Of those that a mesh axis runs over, the one named last changes fastest.
Arguments:
- layer_input: bfloat16 [8192, 4096], P(('groups', 'dp'), 'tensor'), parts along dimension 0, may hold values from -6 to 6
- out_grads: bfloat16 [2, 8192, 14336], P('pipe', ('groups', 'dp'), 'tensor'), parts along dimension 1, may hold values from -6 to 6
- proj_in: bfloat16 [2, 4096, 64], P('pipe', 'tensor'), may hold values from -0.09375 to 0.09375
- proj_out: bfloat16 [2, 14336, 64], P('pipe', 'tensor'), may hold values from -0.046875 to 0.046875
- queries: float32 [2, 4096, 128], P('pipe', ('tensor', 'dp')), may hold values from -6 to 6
Outputs:
- hessian: float32 [2, 8192, 4096], P('pipe', ('groups', 'tensor', 'dp')), parts along dimension 1
- scores: float32 [8, 128], P('groups'), parts along dimension 0
The draws below stay inside these ranges and needn't reach their ends.
There are 2 independent parts, one for each index of `groups`. The reference program is written for one: setup_inputs(seed, part) draws one part's arguments, and reference() takes and returns one part's arrays. A program takes and returns all parts, laid end to end along the dimension named above; an argument that names none is the same for every part. Nothing has to cross between parts.
All inputs are finite; a program needn't handle non-finite values.
Results may differ from the reference program's by a relative error of at most 0.0084.
Values may be sent and summed in bfloat16 or wider, within the bound.
No kernel may reach another device: no remote copies, remote signals or barrier semaphores. Data moves between devices by JAX's collectives and lax.ppermute only.
A program may use at most 128 MiB of HBM per device.

```python
import jax
import jax.numpy as jnp
from jax import lax

D = 4096
FF = 14336
RANK = 64
MODULES = 2
LEN = 1024
NQ = 128
ITERS = 6
TOKENS = 4096
EXAMPLES = 4


def steps_of(rng, shape, cuts, least, largest):
    loudness = 1.0
    for axis_at, blocks in cuts:
        draws = jax.random.uniform(jax.random.fold_in(jax.random.fold_in(rng, 6), axis_at), (blocks,), jnp.float32, least / len(cuts), largest / len(cuts))
        loudness = loudness * jnp.repeat(jnp.exp(draws), shape[axis_at] // blocks).reshape((-1,) + (1,) * (len(shape) - 1 - axis_at))
    return loudness


def scatter_about(rng, dims, deviation, most, pieces=(), kind=jnp.bfloat16):
    values = deviation * jax.random.normal(rng, dims, jnp.float32)
    if pieces:
        values = values * steps_of(rng, dims, pieces, -0.22, 0.18)
    return jnp.clip(values, -most, most).astype(kind)


def setup_inputs(seed: int = 0, part: int = 0) -> dict:
    streams_of = jax.random.split(jax.random.key(seed), 6)
    part_keys = jax.random.split(jax.random.fold_in(streams_of[5], part), 6)
    return {
        "layer_input": scatter_about(part_keys[0], (TOKENS, D), 1.0, 6.0, ((0, 2), (1, 4))),
        "out_grads": scatter_about(part_keys[1], (MODULES, TOKENS, FF), 1.0, 6.0, ((0, 2), (1, 2), (2, 4))),
        "proj_in": scatter_about(streams_of[2], (MODULES, D, RANK), D ** -0.5, 0.09375, ((0, 2), (1, 4))),
        "proj_out": scatter_about(streams_of[3], (MODULES, FF, RANK), FF ** -0.5, 0.046875, ((0, 2), (1, 4))),
        "queries": scatter_about(streams_of[4], (MODULES, RANK * RANK, NQ), 1.0, 6.0, ((0, 2), (1, 8)), jnp.float32),
    }


damping = 0.1


def solve_columns(hessian, rhs):
    highest = lax.Precision.HIGHEST
    solution = jnp.zeros_like(rhs)
    residual = rhs
    direction = rhs
    norm_now = jnp.sum(residual * residual, axis=0)
    for step in range(ITERS):
        image = jnp.dot(hessian, direction, precision=highest)
        alpha = norm_now / jnp.sum(direction * image, axis=0)
        solution = solution + alpha * direction
        residual = residual - alpha * image
        norm_next = jnp.sum(residual * residual, axis=0)
        direction = residual + (norm_next / norm_now) * direction
        norm_now = norm_next
    return solution


def reference(layer_input, out_grads, proj_in, proj_out, queries):
    highest = lax.Precision.HIGHEST
    width = RANK * RANK
    hessians = []
    total = jnp.zeros((EXAMPLES, NQ), jnp.float32)
    for module in range(MODULES):
        xproj = jnp.dot(layer_input, proj_in[module], preferred_element_type=jnp.float32).astype(jnp.bfloat16)
        gproj = jnp.dot(out_grads[module], proj_out[module], preferred_element_type=jnp.float32).astype(jnp.bfloat16)

        def one_example(gram, index):
            start = (index * LEN).astype(jnp.int32)
            xs = lax.dynamic_slice_in_dim(xproj, start, LEN, 0)
            gs = lax.dynamic_slice_in_dim(gproj, start, LEN, 0)
            vectors = (xs[:, :, None] * gs[:, None, :]).reshape(LEN, width).astype(jnp.float32)
            gram = gram + jnp.dot(vectors.T, vectors, precision=highest)
            return gram, jnp.sum(vectors, axis=0) / LEN

        gram, grads = lax.scan(one_example, jnp.zeros((width, width), jnp.float32), jnp.arange(EXAMPLES, dtype=jnp.int32))
        hessian = gram / TOKENS + damping * jnp.eye(width, dtype=jnp.float32)
        solution = solve_columns(hessian, queries[module])
        total = total + jnp.dot(grads, solution, precision=highest)
        hessians.append(hessian)
    return jnp.stack(hessians), total
```

```python
import functools

import jax
import jax.numpy as jnp
from jax import lax
from jax.experimental import pallas as pl
from jax.experimental.pallas import tpu as pltpu
from jax.sharding import PartitionSpec as P

LEN = 1024
ITERS = 6
DAMPING = 0.1
NT = (((1,), (1,)), ((), ()))
VMEM_BYTES = 56 * 1024 * 1024


def whole_spec(shape):
    zeros = (0,) * len(shape)
    return pl.BlockSpec(shape, lambda *_: zeros)


def swap(value, axes, size, offset):
    return lax.ppermute(value, axes, [(i, i ^ offset) for i in range(size)])


def project_kernel(place, inputs, grads, proj_in, proj_out, *outs):
    step = pl.program_id(0)
    x = jnp.dot(inputs[...], proj_in[...], preferred_element_type=jnp.float32)
    g = jnp.dot(grads[...], proj_out[...], preferred_element_type=jnp.float32)
    both = jnp.concatenate([x, g], axis=1).T
    for k, out in enumerate(outs):

        @pl.when(step == k)
        def _():
            out[...] = both


def project(place, inputs, grads, proj_in, proj_out, chunk, block):
    parts = lax.axis_size("tensor")
    features, rank = proj_in.shape
    hidden = proj_out.shape[0]

    def rows(step, place):
        return (chunk * parts + lax.bitwise_xor(step, place[0]), 0)

    shape = (2 * rank, block)
    return pl.pallas_call(
        project_kernel,
        grid_spec=pltpu.PrefetchScalarGridSpec(
            num_scalar_prefetch=1,
            grid=(parts,),
            in_specs=[
                pl.BlockSpec((block, features), rows),
                pl.BlockSpec((block, hidden), rows),
                whole_spec(proj_in.shape),
                whole_spec(proj_out.shape),
            ],
            out_specs=[whole_spec(shape)] * parts,
        ),
        out_shape=[jax.ShapeDtypeStruct(shape, jnp.float32)] * parts,
        compiler_params=pltpu.CompilerParams(vmem_limit_bytes=VMEM_BYTES),
        cost_estimate=pl.CostEstimate(
            flops=2 * parts * block * (features + hidden) * rank,
            bytes_accessed=2 * parts * block * (features + hidden),
            transcendentals=0,
        ),
        name="project",
    )(place, inputs, grads, proj_in, proj_out)


def split_queries_kernel(place, queries, *rest):
    outs, turned = rest[:-1], rest[-1]
    cols, mine, rank = outs[0].shape
    for i in range(mine):
        turned[:, i, :] = queries[i * rank : (i + 1) * rank, :].T
    for k, out in enumerate(outs):
        out[...] = turned[pl.ds(lax.bitwise_xor(place[0], k) * cols, cols)]


def split_queries(place, queries, owners, rank):
    rows, total = queries.shape
    shape = (total // owners, rows // rank, rank)
    return pl.pallas_call(
        split_queries_kernel,
        in_specs=[pl.BlockSpec(memory_space=pltpu.SMEM), pl.BlockSpec(memory_space=pltpu.VMEM)],
        out_specs=[pl.BlockSpec(memory_space=pltpu.VMEM)] * owners,
        out_shape=[jax.ShapeDtypeStruct(shape, jnp.float32)] * owners,
        scratch_shapes=[pltpu.VMEM((total, rows // rank, rank), jnp.float32)],
        compiler_params=pltpu.CompilerParams(vmem_limit_bytes=VMEM_BYTES),
        name="split_queries",
    )(place, queries)


def solve_kernel(tokens, groups, nblocks, place, *refs):
    blocks = refs[:nblocks]
    rest = refs[nblocks:]
    x_s, g_s, pair, direction, residual, image, sums = rest[-7:]
    out = rest[-8]
    queries = rest[:-8]
    cols, side, rank = direction.shape
    mine = side // len(queries)
    block = x_s.shape[2]
    per_group = nblocks // groups
    for n in range(nblocks):
        x_s[n] = blocks[n][:rank, :].astype(jnp.float32)
        g = blocks[n][rank:, :]
        g_s[n] = jnp.concatenate([g, g], axis=0)
    for k, part in enumerate(queries):
        first = pl.multiple_of(lax.bitwise_xor(place[0], k) * mine, mine)
        direction[:, pl.ds(first, mine), :] = part[...]
    residual[...] = direction[...]

    def total(value):
        return jnp.sum(jnp.sum(value, axis=1, keepdims=True), axis=2, keepdims=True)

    def forward(n):
        w = jnp.dot(pair[...], g_s[n], preferred_element_type=jnp.float32)
        x = x_s[n][None]
        u = jnp.sum(w.reshape(cols, side, block) * x, axis=1, keepdims=True)
        sums[n // per_group] += jnp.sum(u, axis=2, keepdims=True)
        return u, x

    def prepare():
        d = direction[...]
        high = d.astype(jnp.bfloat16)
        low = (d - high.astype(jnp.float32)).astype(jnp.bfloat16)
        pair[...] = jnp.concatenate([high, low], axis=2).reshape(cols * side, 2 * rank)
        sums[...] = jnp.zeros_like(sums)
        return total(d * d)

    def step_size(norm, length, energy):
        return norm / (energy * (1.0 / tokens) + DAMPING * length)

    out[...] = jnp.zeros_like(out)

    def one_step(_, norm):
        length = prepare()
        image[...] = jnp.zeros_like(image)

        def one_block(n, energy):
            u, x = forward(n)
            spread = (u * x).astype(jnp.bfloat16).reshape(cols * side, block)
            image[...] += lax.dot_general(
                spread, g_s[n, :rank, :], NT, preferred_element_type=jnp.float32
            ).reshape(cols, side, rank)
            return energy + jnp.sum(u * u, axis=2, keepdims=True)

        energy = lax.fori_loop(0, nblocks, one_block, jnp.zeros_like(norm))
        alpha = step_size(norm, length, energy)
        out[...] += alpha[None] * sums[...]
        d = direction[...]
        r = residual[...] - alpha * (image[...] * (1.0 / tokens) + DAMPING * d)
        residual[...] = r
        later = total(r * r)
        direction[...] = r + later / norm * d
        return later

    norm = lax.fori_loop(0, ITERS - 1, one_step, total(residual[...] * residual[...]))
    length = prepare()

    def last_block(n, energy):
        u, _ = forward(n)
        return energy + jnp.sum(u * u, axis=2, keepdims=True)

    energy = lax.fori_loop(0, nblocks, last_block, jnp.zeros_like(norm))
    out[...] += step_size(norm, length, energy)[None] * sums[...]


def solve(place, blocks, queries, tokens, groups):
    cols, mine, rank = queries[0].shape
    side = mine * len(queries)
    block = blocks[0].shape[1]
    count = len(blocks)
    vectors = pltpu.VMEM((cols, side, rank), jnp.float32)
    return pl.pallas_call(
        functools.partial(solve_kernel, tokens, groups, count),
        in_specs=[pl.BlockSpec(memory_space=pltpu.SMEM)]
        + [pl.BlockSpec(memory_space=pltpu.VMEM)] * (count + len(queries)),
        out_specs=pl.BlockSpec(memory_space=pltpu.VMEM),
        out_shape=jax.ShapeDtypeStruct((groups, cols, 1, 128), jnp.float32),
        scratch_shapes=[
            pltpu.VMEM((count, rank, block), jnp.float32),
            pltpu.VMEM((count, 2 * rank, block), jnp.bfloat16),
            pltpu.VMEM((cols * side, 2 * rank), jnp.bfloat16),
            vectors,
            vectors,
            vectors,
            pltpu.VMEM((groups, cols, 1, 128), jnp.float32),
        ],
        compiler_params=pltpu.CompilerParams(vmem_limit_bytes=VMEM_BYTES),
        cost_estimate=pl.CostEstimate(
            flops=2 * 2 * ITERS * 4 * tokens * cols * side * rank,
            bytes_accessed=4 * tokens * rank,
            transcendentals=0,
        ),
        name="solve",
    )(place, *blocks, *queries)


def hessian_kernel(tokens, count, place, *refs):
    blocks = refs[:count]
    out, x_s, g_s, own, other = refs[count:]
    step = pl.program_id(0)
    rank = x_s.shape[0]
    block = blocks[0].shape[1]
    rows, columns = out.shape

    def vectors(i):
        return (x_s[pl.ds(i, 1), :] * g_s[...]).astype(jnp.bfloat16)

    @pl.when(step == 0)
    def _():
        for n in range(count):
            x_s[:, n * block : (n + 1) * block] = blocks[n][:rank, :].astype(jnp.float32)
            g_s[:, n * block : (n + 1) * block] = blocks[n][rank:, :].astype(jnp.float32)
        for i in range(rows // rank):
            own[i * rank : (i + 1) * rank, :] = vectors(place[0] * (rows // rank) + i)

    for j in range(columns // rank):
        other[j * rank : (j + 1) * rank, :] = vectors(step * (columns // rank) + j)
    gram = lax.dot_general(own[...], other[...], NT, preferred_element_type=jnp.float32)
    row = lax.broadcasted_iota(jnp.int32, (rows, columns), 0) + place[0] * rows
    column = lax.broadcasted_iota(jnp.int32, (rows, columns), 1) + step * columns
    out[...] = gram * (1.0 / tokens) + jnp.where(row == column, DAMPING, 0.0)


def hessian_rows(place, blocks, tokens, rows):
    rank, block = blocks[0].shape[0] // 2, blocks[0].shape[1]
    count = len(blocks)
    width = rank * rank
    columns = 256
    return pl.pallas_call(
        functools.partial(hessian_kernel, tokens, count),
        grid=(width // columns,),
        in_specs=[pl.BlockSpec(memory_space=pltpu.SMEM)]
        + [whole_spec(blocks[0].shape)] * count,
        out_specs=pl.BlockSpec((rows, columns), lambda step: (0, step)),
        out_shape=jax.ShapeDtypeStruct((rows, width), jnp.float32),
        scratch_shapes=[
            pltpu.VMEM((rank, count * block), jnp.float32),
            pltpu.VMEM((rank, count * block), jnp.float32),
            pltpu.VMEM((rows, count * block), jnp.bfloat16),
            pltpu.VMEM((columns, count * block), jnp.bfloat16),
        ],
        compiler_params=pltpu.CompilerParams(vmem_limit_bytes=VMEM_BYTES),
        cost_estimate=pl.CostEstimate(
            flops=2 * rows * width * tokens,
            bytes_accessed=4 * rows * width,
            transcendentals=0,
        ),
        name="hessian_rows",
    )(place, *blocks)


def shards(layer_input, out_grads, proj_in, proj_out, queries):
    rank = proj_in.shape[2]
    parts, dp_size, pipe_size = (lax.axis_size(a) for a in ("tensor", "dp", "pipe"))
    owners = parts * dp_size
    tok_dev = layer_input.shape[0]
    owned, nq = queries.shape[1:]
    tensor_pos = lax.axis_index("tensor").astype(jnp.int32)
    dp_pos = lax.axis_index("dp").astype(jnp.int32)
    owner = tensor_pos * dp_size + dp_pos
    tensor_place = tensor_pos.reshape(1)
    owner_place = owner.reshape(1)
    chunks = 2 if tok_dev // (2 * parts) >= 128 else 1
    block = tok_dev // (chunks * parts)
    tokens = tok_dev * dp_size

    mine = split_queries(owner_place, queries[0], owners, rank)
    columns = [mine[0]] + [swap(mine[k], ("tensor", "dp"), owners, k) for k in range(1, owners)]

    gathered = []
    for chunk in range(chunks):
        partial = project(
            tensor_place, layer_input, out_grads[0], proj_in[0], proj_out[0], chunk, block
        )
        summed = partial[0]
        for k in range(1, parts):
            summed = summed + swap(partial[k], "tensor", parts, k)
        summed = summed.astype(jnp.bfloat16)
        near = [summed] + [swap(summed, "tensor", parts, k) for k in range(1, parts)]
        gathered.append(near)
        for k in range(1, dp_size):
            gathered.append([swap(piece, "dp", dp_size, k) for piece in near])

    blocks = [piece for near in gathered for piece in near]
    groups = len(gathered) if tok_dev // chunks <= LEN else len(blocks)
    each = len(blocks) // groups
    sums = solve(owner_place, blocks, columns, tokens, groups)[:, :, 0, 0]

    example = []
    for g in range(groups):
        chunk, rest = divmod(g * each, dp_size * parts)
        apart, k = divmod(rest, parts)
        first = chunk * parts * block
        if each == 1:
            first = first + (tensor_pos ^ k) * block
        example.append((dp_pos ^ apart) * (tok_dev // LEN) + first // LEN)
    examples = dp_size * tok_dev // LEN
    onehot = jnp.stack(example)[None, :] == jnp.arange(examples, dtype=jnp.int32)[:, None]
    local = jnp.sum(jnp.where(onehot[:, :, None], sums[None], 0.0), axis=1) / LEN
    cols = nq // owners
    placed = lax.dynamic_update_slice(
        jnp.zeros((examples, nq), jnp.float32), local, (jnp.int32(0), owner * cols)
    )
    axes = ("tensor", "dp", "pipe")
    devices = owners * pipe_size
    if devices <= 16:
        scores = placed
        for k in range(1, devices):
            scores = scores + swap(placed, axes, devices, k)
    else:
        scores = lax.psum(placed, axes)
    hessian = hessian_rows(owner_place, blocks, tokens, owned)
    return (hessian[None], scores)


def solution(mesh):
    in_specs = (
        P(("groups", "dp"), "tensor"),
        P("pipe", ("groups", "dp"), "tensor"),
        P("pipe", "tensor", None),
        P("pipe", "tensor", None),
        P("pipe", ("tensor", "dp"), None),
    )
    out_specs = (P("pipe", ("groups", "tensor", "dp"), None), P("groups", None))
    return jax.shard_map(shards, mesh=mesh, in_specs=in_specs, out_specs=out_specs, check_vma=False)
```

```python
import functools

import jax
import jax.numpy as jnp
from jax import lax
from jax.experimental import pallas as pl
from jax.experimental.pallas import tpu as pltpu
from jax.sharding import PartitionSpec as P

LEN = 1024
ITERS = 6
DAMPING = 0.1
NT = (((1,), (1,)), ((), ()))
VMEM_BYTES = 56 * 1024 * 1024


def whole_spec(shape):
    zeros = (0,) * len(shape)
    return pl.BlockSpec(shape, lambda *_: zeros)


def swap(value, axes, size, offset):
    return lax.ppermute(value, axes, [(i, i ^ offset) for i in range(size)])


def encode(value):
    return (value * jnp.abs(value)).astype(jnp.bfloat16)


def decode(code):
    wide = code.astype(jnp.float32)
    root = jnp.sqrt(jnp.abs(wide))
    return jnp.where(wide < 0, -root, root)


def project_kernel(inputs, grads, proj_in, proj_out, out):
    x = lax.dot_general(inputs[...], proj_in[...], NT, preferred_element_type=jnp.float32)
    g = lax.dot_general(grads[...], proj_out[...], NT, preferred_element_type=jnp.float32)
    out[0] = encode(jnp.concatenate([x, g], axis=1).T)


def project(inputs, grads, proj_in, proj_out, chunk, block):
    parts = lax.axis_size("tensor")
    rank, features = proj_in.shape
    hidden = proj_out.shape[1]

    def rows(step):
        return (chunk * parts + step, 0)

    return pl.pallas_call(
        project_kernel,
        grid=(parts,),
        in_specs=[
            pl.BlockSpec((block, features), rows),
            pl.BlockSpec((block, hidden), rows),
            whole_spec(proj_in.shape),
            whole_spec(proj_out.shape),
        ],
        out_specs=pl.BlockSpec((1, 2 * rank, block), lambda step: (step, 0, 0)),
        out_shape=jax.ShapeDtypeStruct((parts, 2 * rank, block), jnp.bfloat16),
        compiler_params=pltpu.CompilerParams(vmem_limit_bytes=VMEM_BYTES),
        cost_estimate=pl.CostEstimate(
            flops=2 * parts * block * (features + hidden) * rank,
            bytes_accessed=2 * parts * block * (features + hidden),
            transcendentals=0,
        ),
        name="project",
    )(inputs, grads, proj_in, proj_out)


def split_queries_kernel(queries, out):
    owners, cols, mine, rank = out.shape
    for i in range(mine):
        turned = queries[i * rank : (i + 1) * rank, :].T
        out[:, :, i, :] = turned.reshape(owners, cols, rank)


def split_queries(queries, owners, rank):
    rows, total = queries.shape
    shape = (owners, total // owners, rows // rank, rank)
    return pl.pallas_call(
        split_queries_kernel,
        out_shape=jax.ShapeDtypeStruct(shape, jnp.float32),
        compiler_params=pltpu.CompilerParams(vmem_limit_bytes=VMEM_BYTES),
        name="split_queries",
    )(queries)


def solve_kernel(tokens, span, count, *refs):
    pieces = refs[:count]
    queries, out, x_s, g_s, pair, direction, residual, image, sums = refs[count:]
    cols, side, rank = direction.shape
    chunks, _, wide = x_s.shape
    parts, _, block = pieces[0].shape
    for n in range(count * parts):
        piece = pieces[n // parts]
        c, at = divmod(n * block, wide)
        x_s[c, :, at : at + block] = piece[n % parts, :rank, :].astype(jnp.float32)
        g = piece[n % parts, rank:, :]
        g_s[c, :rank, at : at + block] = g
        g_s[c, rank:, at : at + block] = g
    mine = queries.shape[2]
    for k in range(side // mine):
        direction[:, k * mine : (k + 1) * mine, :] = queries[k]
    residual[...] = direction[...]

    def total(value):
        return jnp.sum(jnp.sum(value, axis=1, keepdims=True), axis=2, keepdims=True)

    def forward(c):
        w = jnp.dot(pair[...], g_s[c], preferred_element_type=jnp.float32)
        x = x_s[c][None]
        return jnp.sum(w.reshape(cols, side, wide) * x, axis=1, keepdims=True), x

    def prepare():
        d = direction[...]
        high = d.astype(jnp.bfloat16)
        low = (d - high.astype(jnp.float32)).astype(jnp.bfloat16)
        pair[...] = jnp.concatenate([high, low], axis=2).reshape(cols * side, 2 * rank)
        sums[...] = jnp.zeros_like(sums)
        return total(d * d)

    def step_size(norm, length, energy):
        energy = jnp.sum(energy, axis=2, keepdims=True)
        return norm / (energy * (1.0 / tokens) + DAMPING * length)

    def fold(c, u):
        sums[c * wide // span] += jnp.sum(u, axis=2, keepdims=True)

    out[...] = jnp.zeros_like(out)

    def one_step(_, norm):
        length = prepare()
        energy = jnp.zeros((cols, 1, wide), jnp.float32)
        for c in range(chunks):
            u, x = forward(c)
            spread = (u * x).astype(jnp.bfloat16).reshape(cols * side, wide)
            part = lax.dot_general(
                spread, g_s[c, :rank, :], NT, preferred_element_type=jnp.float32
            ).reshape(cols, side, rank)
            image[...] = part if c == 0 else image[...] + part
            fold(c, u)
            energy = energy + u * u
        alpha = step_size(norm, length, energy)
        out[...] += alpha[None] * sums[...]
        d = direction[...]
        r = residual[...] - alpha * (image[...] * (1.0 / tokens) + DAMPING * d)
        residual[...] = r
        later = total(r * r)
        direction[...] = r + later / norm * d
        return later

    norm = lax.fori_loop(0, ITERS - 1, one_step, total(residual[...] * residual[...]))
    length = prepare()
    energy = jnp.zeros((cols, 1, wide), jnp.float32)
    for c in range(chunks):
        u, _ = forward(c)
        fold(c, u)
        energy = energy + u * u
    out[...] += step_size(norm, length, energy)[None] * sums[...]


def solve(pieces, queries, tokens, span):
    owners, cols, mine, rank = queries.shape
    side = mine * owners
    wide = min(512, span)
    count = len(pieces)
    vectors = pltpu.VMEM((cols, side, rank), jnp.float32)
    sums = (tokens // span, cols, 1, 128)
    return pl.pallas_call(
        functools.partial(solve_kernel, tokens, span, count),
        out_shape=jax.ShapeDtypeStruct(sums, jnp.float32),
        scratch_shapes=[
            pltpu.VMEM((tokens // wide, rank, wide), jnp.float32),
            pltpu.VMEM((tokens // wide, 2 * rank, wide), jnp.bfloat16),
            pltpu.VMEM((cols * side, 2 * rank), jnp.bfloat16),
            vectors,
            vectors,
            vectors,
            pltpu.VMEM(sums, jnp.float32),
        ],
        compiler_params=pltpu.CompilerParams(vmem_limit_bytes=VMEM_BYTES),
        cost_estimate=pl.CostEstimate(
            flops=2 * 2 * ITERS * 4 * tokens * cols * side * rank,
            bytes_accessed=4 * tokens * rank,
            transcendentals=0,
        ),
        name="solve",
    )(*pieces, queries)


def hessian_kernel(tokens, count, place, *refs):
    pieces = refs[:count]
    out, x_s, g_s, own, even, odd = refs[count:]
    step = pl.program_id(0)
    steps = pl.num_programs(0)
    rank = x_s.shape[0]
    parts, _, block = pieces[0].shape
    rows = out.shape[0]
    columns = even.shape[0]

    def vectors(i):
        return x_s[pl.ds(i, 1), :].astype(jnp.bfloat16) * g_s[...]

    def form(target, tile):
        for j in range(columns // rank):
            target[j * rank : (j + 1) * rank, :] = vectors(tile * (columns // rank) + j)

    def product(source, half):
        gram = lax.dot_general(own[...], source[...], NT, preferred_element_type=jnp.float32)
        shape = (rows, columns)
        row = lax.broadcasted_iota(jnp.int32, shape, 0) + place[0] * rows
        column = lax.broadcasted_iota(jnp.int32, shape, 1) + (2 * step + half) * columns
        value = gram * (1.0 / tokens) + jnp.where(row == column, DAMPING, 0.0)
        out[:, half * columns : (half + 1) * columns] = value

    @pl.when(step == 0)
    def _():
        for n in range(count * parts):
            piece = pieces[n // parts]
            at = slice(n * block, (n + 1) * block)
            x_s[:, at] = piece[n % parts, :rank, :].astype(jnp.float32)
            g_s[:, at] = piece[n % parts, rank:, :]
        for i in range(rows // rank):
            own[i * rank : (i + 1) * rank, :] = vectors(place[0] * (rows // rank) + i)
        form(even, 0)

    form(odd, 2 * step + 1)
    product(even, 0)
    form(even, lax.rem(2 * step + 2, 2 * steps))
    product(odd, 1)


def hessian_rows(place, pieces, tokens, rows):
    rank = pieces[0].shape[1] // 2
    count = len(pieces)
    width = rank * rank
    columns = 256
    return pl.pallas_call(
        functools.partial(hessian_kernel, tokens, count),
        grid=(width // (2 * columns),),
        in_specs=[pl.BlockSpec(memory_space=pltpu.SMEM)]
        + [whole_spec(pieces[0].shape)] * count,
        out_specs=pl.BlockSpec((rows, 2 * columns), lambda step: (0, step)),
        out_shape=jax.ShapeDtypeStruct((rows, width), jnp.float32),
        scratch_shapes=[
            pltpu.VMEM((rank, tokens), jnp.float32),
            pltpu.VMEM((rank, tokens), jnp.bfloat16),
            pltpu.VMEM((rows, tokens), jnp.bfloat16),
            pltpu.VMEM((columns, tokens), jnp.bfloat16),
            pltpu.VMEM((columns, tokens), jnp.bfloat16),
        ],
        compiler_params=pltpu.CompilerParams(vmem_limit_bytes=VMEM_BYTES),
        cost_estimate=pl.CostEstimate(
            flops=2 * rows * width * tokens,
            bytes_accessed=4 * rows * width,
            transcendentals=0,
        ),
        name="hessian_rows",
    )(place, *pieces)


def shards(layer_input, out_grads, proj_in, proj_out, queries):
    rank = proj_in.shape[2]
    parts, dp_size = lax.axis_size("tensor"), lax.axis_size("dp")
    owners = parts * dp_size
    tok_dev = layer_input.shape[0]
    owned, nq = queries.shape[1:]
    dp_pos = lax.axis_index("dp").astype(jnp.int32)
    owner = lax.axis_index("tensor").astype(jnp.int32) * dp_size + dp_pos
    chunks = 2 if tok_dev // (2 * parts) >= 128 else 1
    block = tok_dev // (chunks * parts)
    tokens = tok_dev * dp_size

    def exchange(value, axes):
        return lax.all_to_all(value, axes, 0, 0, tiled=True)

    split = split_queries(queries[0], owners, rank)
    flat = split.reshape(owners, split.shape[1] * split.shape[2], rank)
    columns = exchange(flat, ("tensor", "dp")).reshape(split.shape)

    pieces, first = [], []
    for chunk in range(chunks):
        partial = project(
            layer_input, out_grads[0], proj_in[0].T, proj_out[0].T, chunk, block
        )
        summed = jnp.sum(decode(exchange(partial, "tensor")), axis=0).astype(jnp.bfloat16)
        near = exchange(jnp.broadcast_to(summed, (parts,) + summed.shape), "tensor")
        for k in range(dp_size):
            pieces.append(near if k == 0 else swap(near, "dp", dp_size, k))
            first.append(((dp_pos ^ k) * tok_dev, chunk * (tok_dev // chunks)))

    span = min(tok_dev // chunks, LEN)
    sums = solve(pieces, columns, tokens, span)[:, :, 0, 0]
    example = []
    for g in range(tokens // span):
        piece, inside = divmod(g * span, tok_dev // chunks)
        away, start = first[piece]
        example.append(away // LEN + (start + inside) // LEN)
    examples = tokens // LEN
    onehot = jnp.stack(example)[None, :] == jnp.arange(examples, dtype=jnp.int32)[:, None]
    local = jnp.sum(jnp.where(onehot[:, :, None], sums[None], 0.0), axis=1) / LEN
    cols = nq // owners
    placed = lax.dynamic_update_slice(
        jnp.zeros((examples, nq), jnp.float32), local, (jnp.int32(0), owner * cols)
    )
    scores = jnp.sum(lax.all_gather(placed, ("tensor", "dp", "pipe"), axis=0), axis=0)
    hessian = hessian_rows(owner.reshape(1), pieces, tokens, owned)
    return (hessian[None], scores)


def solution(mesh):
    in_specs = (
        P(("groups", "dp"), "tensor"),
        P("pipe", ("groups", "dp"), "tensor"),
        P("pipe", "tensor", None),
        P("pipe", "tensor", None),
        P("pipe", ("tensor", "dp"), None),
    )
    out_specs = (P("pipe", ("groups", "tensor", "dp"), None), P("groups", None))
    return jax.shard_map(shards, mesh=mesh, in_specs=in_specs, out_specs=out_specs, check_vma=False)
```

```python
import functools

import jax
import jax.numpy as jnp
from jax import lax
from jax.experimental import pallas as pl
from jax.experimental.pallas import tpu as pltpu
from jax.sharding import PartitionSpec as P

LEN = 1024
ITERS = 6
DAMPING = 0.1
NT = (((1,), (1,)), ((), ()))
VMEM_BYTES = 56 * 1024 * 1024


def whole_spec(shape):
    zeros = (0,) * len(shape)
    return pl.BlockSpec(shape, lambda *_: zeros)


def swap(value, axes, size, offset):
    return lax.ppermute(value, axes, [(i, i ^ offset) for i in range(size)])


def encode(value):
    return (value * jnp.abs(value)).astype(jnp.bfloat16)


def decode(code):
    wide = code.astype(jnp.float32)
    root = jnp.sqrt(jnp.abs(wide))
    return jnp.where(wide < 0, -root, root)


def project_kernel(ways, *refs):
    inputs, grads = refs[:ways], refs[ways : 2 * ways]
    proj_in, proj_out, out = refs[2 * ways :]
    rows = inputs[0].shape[0]
    for w in range(ways):
        x = lax.dot_general(inputs[w][...], proj_in[...], NT, preferred_element_type=jnp.float32)
        g = lax.dot_general(grads[w][...], proj_out[...], NT, preferred_element_type=jnp.float32)
        both = jnp.concatenate([x, g], axis=1).T
        out[0, :, w * rows : (w + 1) * rows] = encode(both)


def project(inputs, grads, proj_in, proj_out, parts):
    rank, features = proj_in.shape
    hidden = proj_out.shape[1]
    tokens = inputs.shape[0]
    block = tokens // parts
    tile = min(block, 256)
    split = block // tile
    ways = tile // 128

    def rows(way):
        return lambda step: (step * ways + way, 0)

    return pl.pallas_call(
        functools.partial(project_kernel, ways),
        grid=(parts * split,),
        in_specs=[pl.BlockSpec((128, features), rows(w)) for w in range(ways)]
        + [pl.BlockSpec((128, hidden), rows(w)) for w in range(ways)]
        + [whole_spec(proj_in.shape), whole_spec(proj_out.shape)],
        out_specs=pl.BlockSpec(
            (1, 2 * rank, tile), lambda step: (step // split, 0, lax.rem(step, split))
        ),
        out_shape=jax.ShapeDtypeStruct((parts, 2 * rank, block), jnp.bfloat16),
        compiler_params=pltpu.CompilerParams(vmem_limit_bytes=VMEM_BYTES),
        cost_estimate=pl.CostEstimate(
            flops=2 * tokens * (features + hidden) * rank,
            bytes_accessed=2 * tokens * (features + hidden),
            transcendentals=0,
        ),
        name="project",
    )(*[inputs] * ways, *[grads] * ways, proj_in, proj_out)


def split_queries_kernel(queries, out):
    owners, rank, width = out.shape
    cols = queries.shape[1] // owners
    for i in range(width // cols):
        rows = queries[i * rank : (i + 1) * rank, :]
        for k in range(owners):
            out[k, :, i * cols : (i + 1) * cols] = rows[:, k * cols : (k + 1) * cols]


def split_queries(queries, owners, rank):
    rows, total = queries.shape
    shape = (owners, rank, (rows // rank) * (total // owners))
    return pl.pallas_call(
        split_queries_kernel,
        out_shape=jax.ShapeDtypeStruct(shape, jnp.float32),
        compiler_params=pltpu.CompilerParams(vmem_limit_bytes=VMEM_BYTES),
        name="split_queries",
    )(queries)


def solve_kernel(tokens, span, count, place, *refs):
    pieces = refs[:count]
    queries, scores, out, x_s, g_s, pair, direction, residual, image, sums = refs[count:]
    cols, side, rank = direction.shape
    chunks, _, wide = x_s.shape
    parts, _, block = pieces[0].shape
    for n in range(count * parts):
        piece = pieces[n // parts]
        c, at = divmod(n * block, wide)
        x_s[c, :, at : at + block] = piece[n % parts, :rank, :].astype(jnp.float32)
        g = piece[n % parts, rank:, :]
        g_s[c, :rank, at : at + block] = g
        g_s[c, rank:, at : at + block] = g
    mine = queries.shape[2] // cols
    for k in range(queries.shape[0]):
        turned = queries[k].T
        for i in range(mine):
            direction[:, k * mine + i, :] = turned[i * cols : (i + 1) * cols, :]
    residual[...] = direction[...]

    def total(value):
        return jnp.sum(jnp.sum(value, axis=1, keepdims=True), axis=2, keepdims=True)

    def forward(c):
        w = jnp.dot(pair[...], g_s[c], preferred_element_type=jnp.float32)
        x = x_s[c][None]
        return jnp.sum(w.reshape(cols, side, wide) * x, axis=1, keepdims=True), x

    def prepare():
        d = direction[...]
        high = d.astype(jnp.bfloat16)
        low = (d - high.astype(jnp.float32)).astype(jnp.bfloat16)
        pair[...] = jnp.concatenate([high, low], axis=2).reshape(cols * side, 2 * rank)
        sums[...] = jnp.zeros_like(sums)
        return total(d * d)

    def step_size(norm, length, energy):
        energy = jnp.sum(energy, axis=2, keepdims=True)
        return norm / (energy * (1.0 / tokens) + DAMPING * length)

    def fold(c, u):
        sums[c * wide // span] += jnp.sum(u, axis=2, keepdims=True)

    out[...] = jnp.zeros_like(out)

    def one_step(_, norm):
        length = prepare()
        energy = jnp.zeros((cols, 1, wide), jnp.float32)
        for c in range(chunks):
            u, x = forward(c)
            spread = (u * x).astype(jnp.bfloat16).reshape(cols * side, wide)
            part = lax.dot_general(
                spread, g_s[c, :rank, :], NT, preferred_element_type=jnp.float32
            ).reshape(cols, side, rank)
            image[...] = part if c == 0 else image[...] + part
            fold(c, u)
            energy = energy + u * u
        alpha = step_size(norm, length, energy)
        out[...] += alpha[None] * sums[...]
        d = direction[...]
        r = residual[...] - alpha * (image[...] * (1.0 / tokens) + DAMPING * d)
        residual[...] = r
        later = total(r * r)
        direction[...] = r + later / norm * d
        return later

    norm = lax.fori_loop(0, ITERS - 1, one_step, total(residual[...] * residual[...]))
    length = prepare()
    energy = jnp.zeros((cols, 1, wide), jnp.float32)
    for c in range(chunks):
        u, _ = forward(c)
        fold(c, u)
        energy = energy + u * u
    out[...] += step_size(norm, length, energy)[None] * sums[...]

    scores[...] = jnp.zeros_like(scores)
    lane = lax.broadcasted_iota(jnp.int32, (cols, 1, 128), 2)
    column = lax.broadcasted_iota(jnp.int32, (cols, 1, 128), 0) + place[0] * cols
    for n in range(tokens // span):
        row = jnp.sum(jnp.where(lane == column, out[n], 0.0), axis=0) * (1.0 / LEN)
        at = pl.ds(place[1 + n], 1)
        scores[0, at, :] += row
    for k in range(1, scores.shape[0]):
        scores[k] = scores[0]


def solve(place, pieces, queries, tokens, span, devices):
    owners, rank, width = queries.shape
    side = rank
    cols = owners * width // side
    wide = min(512, span)
    count = len(pieces)
    vectors = pltpu.VMEM((cols, side, rank), jnp.float32)
    sums = (tokens // span, cols, 1, 128)
    return pl.pallas_call(
        functools.partial(solve_kernel, tokens, span, count),
        in_specs=[pl.BlockSpec(memory_space=pltpu.SMEM)]
        + [pl.BlockSpec(memory_space=pltpu.VMEM)] * (count + 1),
        out_specs=pl.BlockSpec(memory_space=pltpu.VMEM),
        out_shape=jax.ShapeDtypeStruct((devices, tokens // LEN, 128), jnp.float32),
        scratch_shapes=[
            pltpu.VMEM(sums, jnp.float32),
            pltpu.VMEM((tokens // wide, rank, wide), jnp.float32),
            pltpu.VMEM((tokens // wide, 2 * rank, wide), jnp.bfloat16),
            pltpu.VMEM((cols * side, 2 * rank), jnp.bfloat16),
            vectors,
            vectors,
            vectors,
            pltpu.VMEM(sums, jnp.float32),
        ],
        compiler_params=pltpu.CompilerParams(vmem_limit_bytes=VMEM_BYTES),
        cost_estimate=pl.CostEstimate(
            flops=2 * 2 * ITERS * 4 * tokens * cols * side * rank,
            bytes_accessed=4 * tokens * rank,
            transcendentals=0,
        ),
        name="solve",
    )(place, *pieces, queries)


def hessian_kernel(tokens, count, first, last, place, *refs):
    pieces = refs[:count]
    before = None if first else refs[count]
    out, x_s, g_s, own, even, odd = refs[-6:]
    step = pl.program_id(0)
    steps = pl.num_programs(0)
    rank = x_s.shape[0]
    parts, _, block = pieces[0].shape
    rows = out.shape[0]
    columns = even.shape[0]

    def vectors(i):
        return x_s[pl.ds(i, 1), :].astype(jnp.bfloat16) * g_s[...]

    def form(target, tile):
        for j in range(columns // rank):
            target[j * rank : (j + 1) * rank, :] = vectors(tile * (columns // rank) + j)

    def product(source, half):
        at = slice(half * columns, (half + 1) * columns)
        gram = lax.dot_general(own[...], source[...], NT, preferred_element_type=jnp.float32)
        if not first:
            gram = gram + before[:, at]
        if last:
            shape = (rows, columns)
            row = lax.broadcasted_iota(jnp.int32, shape, 0) + place[0] * rows
            column = lax.broadcasted_iota(jnp.int32, shape, 1) + (2 * step + half) * columns
            gram = gram * (1.0 / tokens) + jnp.where(row == column, DAMPING, 0.0)
        out[:, at] = gram

    @pl.when(step == 0)
    def _():
        for n in range(count * parts):
            piece = pieces[n // parts]
            at = slice(n * block, (n + 1) * block)
            x_s[:, at] = piece[n % parts, :rank, :].astype(jnp.float32)
            g_s[:, at] = piece[n % parts, rank:, :]
        for i in range(rows // rank):
            own[i * rank : (i + 1) * rank, :] = vectors(place[0] * (rows // rank) + i)
        form(even, 0)

    form(odd, 2 * step + 1)
    product(even, 0)
    form(even, lax.rem(2 * step + 2, 2 * steps))
    product(odd, 1)


def hessian_rows(place, pieces, tokens, rows, before, last):
    rank = pieces[0].shape[1] // 2
    count = len(pieces)
    width = rank * rank
    columns = 256
    here = count * pieces[0].shape[0] * pieces[0].shape[2]
    first = before is None
    tile = pl.BlockSpec((rows, 2 * columns), lambda step: (0, step))
    return pl.pallas_call(
        functools.partial(hessian_kernel, tokens, count, first, last),
        grid=(width // (2 * columns),),
        in_specs=[pl.BlockSpec(memory_space=pltpu.SMEM)]
        + [whole_spec(pieces[0].shape)] * count
        + ([] if first else [tile]),
        out_specs=tile,
        out_shape=jax.ShapeDtypeStruct((rows, width), jnp.float32),
        scratch_shapes=[
            pltpu.VMEM((rank, here), jnp.float32),
            pltpu.VMEM((rank, here), jnp.bfloat16),
            pltpu.VMEM((rows, here), jnp.bfloat16),
            pltpu.VMEM((columns, here), jnp.bfloat16),
            pltpu.VMEM((columns, here), jnp.bfloat16),
        ],
        input_output_aliases={} if first else {1 + count: 0},
        compiler_params=pltpu.CompilerParams(vmem_limit_bytes=VMEM_BYTES),
        cost_estimate=pl.CostEstimate(
            flops=2 * rows * width * here,
            bytes_accessed=(1 if first else 2) * 4 * rows * width,
            transcendentals=0,
        ),
        name="hessian_first" if first else "hessian_rest",
    )(place, *pieces, *([] if first else [before]))


def shards(layer_input, out_grads, proj_in, proj_out, queries):
    rank = proj_in.shape[2]
    parts, dp_size, pipe_size = (lax.axis_size(a) for a in ("tensor", "dp", "pipe"))
    owners = parts * dp_size
    tok_dev = layer_input.shape[0]
    owned = queries.shape[1]
    dp_pos = lax.axis_index("dp").astype(jnp.int32)
    owner = lax.axis_index("tensor").astype(jnp.int32) * dp_size + dp_pos
    tokens = tok_dev * dp_size

    def exchange(value, axes):
        return lax.all_to_all(value, axes, 0, 0, tiled=True)

    columns = exchange(split_queries(queries[0], owners, rank), ("tensor", "dp"))
    partial = project(layer_input, out_grads[0], proj_in[0].T, proj_out[0].T, parts)
    columns, partial = lax.optimization_barrier((columns, partial))
    summed = jnp.sum(decode(exchange(partial, "tensor")), axis=0).astype(jnp.bfloat16)
    near = exchange(jnp.broadcast_to(summed, (parts,) + summed.shape), "tensor")
    far = [swap(near, "dp", dp_size, k) for k in range(1, dp_size)]

    span = min(tok_dev, LEN)
    rows = [
        (dp_pos ^ k) * (tok_dev // LEN) + at * span // LEN
        for k in range(dp_size)
        for at in range(tok_dev // span)
    ]
    place = jnp.stack([owner] + rows)

    begun = hessian_rows(place, [near], tokens, owned, None, not far)
    if far:
        begun, *far = lax.optimization_barrier((begun, *far))
    shares = solve(place, [near, *far], columns, tokens, span, owners * pipe_size)
    scores = jnp.sum(exchange(shares, ("tensor", "dp", "pipe")), axis=0)
    if far:
        begun = hessian_rows(place, far, tokens, owned, begun, True)
    return (begun[None], scores)


def solution(mesh):
    in_specs = (
        P(("groups", "dp"), "tensor"),
        P("pipe", ("groups", "dp"), "tensor"),
        P("pipe", "tensor", None),
        P("pipe", "tensor", None),
        P("pipe", ("tensor", "dp"), None),
    )
    out_specs = (P("pipe", ("groups", "tensor", "dp"), None), P("groups", None))
    return jax.shard_map(shards, mesh=mesh, in_specs=in_specs, out_specs=out_specs, check_vma=False)
```

```python
import functools

import jax
import jax.numpy as jnp
from jax import lax
from jax.experimental import pallas as pl
from jax.experimental.pallas import tpu as pltpu
from jax.sharding import PartitionSpec as P

LEN = 1024
ITERS = 6
DAMPING = 0.1
NT = (((1,), (1,)), ((), ()))
VMEM_BYTES = 56 * 1024 * 1024


def whole_spec(shape):
    zeros = (0,) * len(shape)
    return pl.BlockSpec(shape, lambda *_: zeros)


def swap(value, axes, size, offset):
    return lax.ppermute(value, axes, [(i, i ^ offset) for i in range(size)])


def encode(value):
    return (value * jnp.abs(value)).astype(jnp.bfloat16)


def decode(code):
    wide = code.astype(jnp.float32)
    root = jnp.sqrt(jnp.abs(wide))
    return jnp.where(wide < 0, -root, root)


def order(position, count, first):
    bits = (count - 1).bit_length()
    offset = first
    for b in range(bits):
        bit = lax.shift_right_logical(position, jnp.int32(bits - 1 - b)) & 1
        offset = offset + bit * (2 << b)
    return offset


def project_kernel(sent, count, narrow, place, *refs):
    inputs, grads = refs[:count], refs[count : 2 * count]
    proj_in, proj_out = refs[2 * count : 2 * count + 2]
    rest = refs[2 * count + 2 :]
    queries, out, split, sums = (None, rest[0], None, rest[1]) if sent else rest
    step = pl.program_id(0)
    rank = proj_in.shape[0]

    def product(left, right):
        return lax.dot_general(left[...], right[...], NT, preferred_element_type=jnp.float32)

    @pl.when(step == 0)
    def _():
        sums[...] = jnp.zeros_like(sums)
        if not sent:
            split_queries(queries, split)

    for n in range(count):
        sums[n, rank:, :] += product(proj_out, grads[n])

    @pl.when(step < narrow)
    def _():
        for n in range(count):
            sums[n, :rank, :] += product(proj_in, inputs[n])

    @pl.when(step == pl.num_programs(0) - 1)
    def _():
        out[...] = encode(sums[...]) if sent else sums[...]


def split_queries(queries, out):
    owners, rank, width = out.shape
    cols = queries.shape[1] // owners
    for i in range(width // cols):
        rows = queries[i * rank : (i + 1) * rank, :]
        for k in range(owners):
            out[k, :, i * cols : (i + 1) * cols] = rows[:, k * cols : (k + 1) * cols]


def project(place, inputs, grads, proj_in, proj_out, parts, queries=None, owners=1):
    sent = queries is None
    rank, features = proj_in.shape
    hidden = proj_out.shape[1]
    block = inputs.shape[0] // parts
    count = parts // 2
    depth = next(d for d in (512, 256, 128) if features % d == 0 and hidden % d == 0)
    narrow = features // depth

    def part(n, place):
        return lax.bitwise_xor(place[0], order(jnp.int32(n), count, 1 if sent else 0))

    def chunk(n, last):
        return lambda step, place: (part(n, place), jnp.minimum(step, last))

    wide = [pl.BlockSpec((block, depth), chunk(n, hidden // depth - 1)) for n in range(count)]
    thin = [pl.BlockSpec((block, depth), chunk(n, narrow - 1)) for n in range(count)]
    shape = (count, 2 * rank, block)
    out_shape = [jax.ShapeDtypeStruct(shape, jnp.bfloat16 if sent else jnp.float32)]
    if not sent:
        cut = (owners, rank, queries.size // (rank * owners))
        out_shape.append(jax.ShapeDtypeStruct(cut, jnp.float32))
    return pl.pallas_call(
        functools.partial(project_kernel, sent, count, narrow),
        grid_spec=pltpu.PrefetchScalarGridSpec(
            num_scalar_prefetch=1,
            grid=(hidden // depth,),
            in_specs=thin
            + wide
            + [
                pl.BlockSpec((rank, depth), lambda step, place: (0, jnp.minimum(step, narrow - 1))),
                pl.BlockSpec((rank, depth), lambda step, place: (0, step)),
            ]
            + ([] if sent else [whole_spec(queries.shape)]),
            out_specs=[whole_spec(o.shape) for o in out_shape],
            scratch_shapes=[pltpu.VMEM(shape, jnp.float32)],
        ),
        out_shape=out_shape,
        compiler_params=pltpu.CompilerParams(vmem_limit_bytes=VMEM_BYTES),
        cost_estimate=pl.CostEstimate(
            flops=2 * count * block * (features + hidden) * rank,
            bytes_accessed=2 * count * block * (features + hidden),
            transcendentals=0,
        ),
        name="project_sent" if sent else "project_kept",
    )(
        place,
        *[inputs] * count,
        *[grads] * count,
        proj_in,
        proj_out,
        *([] if sent else [queries]),
    )


def solve_kernel(tokens, count, parts_at, place, apart, *refs):
    pieces = refs[:count]
    queries, scores, kept, x_s, g_s, pair, direction, residual, image, sums = refs[count:]
    side, cols, rank = direction.shape
    chunks, _, wide = x_s.shape
    each, _, block = pieces[0].shape
    owners, _, width = queries.shape
    mine = side // owners
    real = width // mine
    for c in range(chunks):
        n, at = divmod(c * wide, block)
        piece = pieces[n // each]
        x_s[c] = piece[n % each, :rank, at : at + wide].astype(jnp.float32)
        g = piece[n % each, rank:, at : at + wide]
        g_s[c, :rank, :] = g
        g_s[c, rank:, :] = g
    if real < cols:
        direction[...] = jnp.zeros_like(direction)
    for k in range(owners):
        turned = queries[k].T
        for i in range(mine):
            direction[k * mine + i, :real, :] = turned[i * real : (i + 1) * real, :]
    residual[...] = direction[...]
    together = 256 // cols
    groups = side // together
    lanes = [slice(k, k + min(256, wide)) for k in range(0, wide, 256)]

    def total(value):
        return jnp.sum(jnp.sum(value, axis=0), axis=1, keepdims=True)

    def rows(group):
        return slice(group * together * cols, (group + 1) * together * cols)

    def features(group):
        return range(group * together, (group + 1) * together)

    def collect(c, group, us):
        sums_of = []
        for at, u in zip(lanes, us):
            w = jnp.dot(pair[rows(group), :], g_s[c, :, at], preferred_element_type=jnp.float32)
            for n, i in enumerate(features(group)):
                u = u + w[n * cols : (n + 1) * cols, :] * x_s[c, i : i + 1, at]
            sums_of.append(u)
        return sums_of

    def spread(c, group, us):
        part = 0.0
        for at, u in zip(lanes, us):
            terms = [(u * x_s[c, i : i + 1, at]).astype(jnp.bfloat16) for i in features(group)]
            part = part + lax.dot_general(
                g_s[c, :rank, at],
                jnp.concatenate(terms, axis=0),
                NT,
                preferred_element_type=jnp.float32,
            )
        image[:, rows(group)] = part if c == 0 else image[:, rows(group)] + part

    def fold(value):
        width = value[0].shape[1]
        return functools.reduce(
            jnp.add, [v[:, k : k + 128] for v in value for k in range(0, width, 128)]
        )

    def apply(back):
        d = direction[...]
        high = d.astype(jnp.bfloat16)
        low = (d - high.astype(jnp.float32)).astype(jnp.bfloat16)
        pair[...] = jnp.concatenate([high, low], axis=2).reshape(side * cols, 2 * rank)
        energy = jnp.zeros((cols, 128), jnp.float32)
        zeros = [jnp.zeros((cols, at.stop - at.start), jnp.float32) for at in lanes]
        later = zeros
        for group in range(groups):
            later = collect(0, group, later)
        for c in range(chunks):
            us, later = later, zeros
            for group in range(groups):
                if c + 1 < chunks:
                    later = collect(c + 1, group, later)
                if back:
                    spread(c, group, us)
            sums[c] = fold(us)
            energy = energy + fold([u * u for u in us])
        return total(d * d), jnp.sum(energy, axis=1, keepdims=True)

    def advance(norm, length, energy):
        alpha = norm / (energy * (1.0 / tokens) + DAMPING * length)
        for c in range(chunks):
            kept[c] += alpha * sums[c]
        return alpha

    kept[...] = jnp.zeros_like(kept)

    def one_step(_, norm):
        alpha = advance(norm, *apply(True))
        d = direction[...]
        turned = image[...].T.reshape(side, cols, rank)
        r = residual[...] - alpha * (turned * (1.0 / tokens) + DAMPING * d)
        residual[...] = r
        later = total(r * r)
        direction[...] = r + later / norm * d
        return later

    norm = lax.fori_loop(0, ITERS - 1, one_step, total(residual[...] * residual[...]))
    advance(norm, *apply(False))

    scores[...] = jnp.zeros_like(scores)
    lane = lax.broadcasted_iota(jnp.int32, (cols, 128), 1)
    column = lax.broadcasted_iota(jnp.int32, (cols, 128), 0)
    owner = place[0] * (owners // parts_at[1]) + apart[0]
    here = (lane == column + owner * real) & (column < real)
    for c in range(chunks):
        n, at = divmod(c * wide, block)
        away, k = parts_at[0][n]
        example = lax.bitwise_xor(apart[0], away) * parts_at[2] + lax.div(
            lax.bitwise_xor(place[0], k) * block + at, LEN
        )
        value = jnp.sum(kept[c], axis=1, keepdims=True) * (1.0 / LEN)
        row = jnp.sum(jnp.where(here, value, 0.0), axis=0, keepdims=True)
        scores[0, pl.ds(example, 1), :] += row
    for k in range(1, scores.shape[0]):
        scores[k] = scores[0]


def solve(place, apart, pieces, where, queries, tokens, examples, parts, devices):
    owners, rank, width = queries.shape
    cols = max(owners * width // rank, 16)
    count, block = len(pieces), pieces[0].shape[2]
    wide = min(512, block)
    chunks = tokens // wide
    vectors = pltpu.VMEM((rank, cols, rank), jnp.float32)
    sums = pltpu.VMEM((chunks, cols, 128), jnp.float32)
    smem = pl.BlockSpec(memory_space=pltpu.SMEM)
    dp_size = owners // parts
    return pl.pallas_call(
        functools.partial(solve_kernel, tokens, count, (where, parts, examples // dp_size)),
        in_specs=[smem, smem] + [pl.BlockSpec(memory_space=pltpu.VMEM)] * (count + 1),
        out_specs=pl.BlockSpec(memory_space=pltpu.VMEM),
        out_shape=jax.ShapeDtypeStruct((devices, examples, 128), jnp.float32),
        scratch_shapes=[
            sums,
            pltpu.VMEM((chunks, rank, wide), jnp.float32),
            pltpu.VMEM((chunks, 2 * rank, wide), jnp.bfloat16),
            pltpu.VMEM((rank * cols, 2 * rank), jnp.bfloat16),
            vectors,
            vectors,
            pltpu.VMEM((rank, rank * cols), jnp.float32),
            sums,
        ],
        compiler_params=pltpu.CompilerParams(vmem_limit_bytes=VMEM_BYTES),
        cost_estimate=pl.CostEstimate(
            flops=2 * 2 * ITERS * 4 * tokens * cols * rank * rank,
            bytes_accessed=4 * tokens * rank,
            transcendentals=0,
        ),
        name="solve",
    )(place, apart, *pieces, queries)


def hessian_kernel(tokens, count, dp_size, first, last, place, apart, *refs):
    pieces = refs[:count]
    before = None if first else refs[count]
    out, x_s, g_s, own, even, odd = refs[-6:]
    step = pl.program_id(0)
    steps = pl.num_programs(0)
    rank = x_s.shape[0]
    each, _, block = pieces[0].shape
    rows = out.shape[0]
    columns = even.shape[0]
    first_row = (place[0] * dp_size + apart[0]) * rows

    def vectors(i):
        return x_s[pl.ds(i, 1), :].astype(jnp.bfloat16) * g_s[...]

    def form(target, tile):
        for j in range(columns // rank):
            target[j * rank : (j + 1) * rank, :] = vectors(tile * (columns // rank) + j)

    def product(source, half):
        at = slice(half * columns, (half + 1) * columns)
        gram = lax.dot_general(own[...], source[...], NT, preferred_element_type=jnp.float32)
        if not first:
            gram = gram + before[:, at]
        if last:
            shape = (rows, columns)
            row = lax.broadcasted_iota(jnp.int32, shape, 0) + first_row
            column = lax.broadcasted_iota(jnp.int32, shape, 1) + (2 * step + half) * columns
            gram = gram * (1.0 / tokens) + jnp.where(row == column, DAMPING, 0.0)
        out[:, at] = gram

    @pl.when(step == 0)
    def _():
        for n in range(count * each):
            at = slice(n * block, (n + 1) * block)
            x_s[:, at] = pieces[n // each][n % each, :rank, :].astype(jnp.float32)
            g_s[:, at] = pieces[n // each][n % each, rank:, :]
        for i in range(rows // rank):
            own[i * rank : (i + 1) * rank, :] = vectors(first_row // rank + i)
        form(even, 0)

    form(odd, 2 * step + 1)
    product(even, 0)
    form(even, lax.rem(2 * step + 2, 2 * steps))
    product(odd, 1)


def hessian_rows(place, apart, dp_size, pieces, tokens, rows, before, last):
    rank = pieces[0].shape[1] // 2
    count = len(pieces)
    width = rank * rank
    columns = 256
    here = count * pieces[0].shape[0] * pieces[0].shape[2]
    first = before is None
    tile = pl.BlockSpec((rows, 2 * columns), lambda step: (0, step))
    return pl.pallas_call(
        functools.partial(hessian_kernel, tokens, count, dp_size, first, last),
        grid=(width // (2 * columns),),
        in_specs=[pl.BlockSpec(memory_space=pltpu.SMEM)] * 2
        + [whole_spec(pieces[0].shape)] * count
        + ([] if first else [tile]),
        out_specs=tile,
        out_shape=jax.ShapeDtypeStruct((rows, width), jnp.float32),
        scratch_shapes=[
            pltpu.VMEM((rank, here), jnp.float32),
            pltpu.VMEM((rank, here), jnp.bfloat16),
            pltpu.VMEM((rows, here), jnp.bfloat16),
            pltpu.VMEM((columns, here), jnp.bfloat16),
            pltpu.VMEM((columns, here), jnp.bfloat16),
        ],
        input_output_aliases={} if first else {2 + count: 0},
        compiler_params=pltpu.CompilerParams(vmem_limit_bytes=VMEM_BYTES),
        cost_estimate=pl.CostEstimate(
            flops=2 * rows * width * here,
            bytes_accessed=(1 if first else 2) * 4 * rows * width,
            transcendentals=0,
        ),
        name="hessian_begin" if first else "hessian_end" if last else "hessian_more",
    )(place, apart, *pieces, *([] if first else [before]))


def shards(layer_input, out_grads, proj_in, proj_out, queries):
    rank = proj_in.shape[2]
    parts, dp_size, pipe_size = (lax.axis_size(a) for a in ("tensor", "dp", "pipe"))
    owners = parts * dp_size
    tok_dev = layer_input.shape[0]
    owned = queries.shape[1]
    place = lax.axis_index("tensor").astype(jnp.int32).reshape(1)
    apart = lax.axis_index("dp").astype(jnp.int32).reshape(1)
    tokens = tok_dev * dp_size

    operands = (place, layer_input, out_grads[0], proj_in[0].T, proj_out[0].T, parts)
    (sent,) = project(*operands)
    sent = swap(sent, "tensor", parts, 1)
    total, cut = project(*operands, queries[0], owners)
    total = total + decode(sent)
    offset = 2
    while 2 * offset < parts:
        half = total.shape[0] // 2
        total = total[:half] + decode(swap(encode(total[half:]), "tensor", parts, offset))
        offset *= 2
    other = decode(swap(encode(total), "tensor", parts, offset))
    near = [jnp.stack([total[0] + other[1], total[1] + other[0]]).astype(jnp.bfloat16)]
    at = [[0, offset]]
    cut, near[0] = lax.optimization_barrier((cut, near[0]))
    columns = lax.all_to_all(cut, ("tensor", "dp"), 0, 0, tiled=True)

    while offset > 1:
        offset //= 2
        if offset < parts // 2:
            near = near + [swap(piece, "tensor", parts, offset) for piece in near]
            at = at + [[k ^ offset for k in ks] for ks in at]
    far = [swap(piece, "dp", dp_size, k) for k in range(1, dp_size) for piece in near]
    where = [(k, part) for k in range(dp_size) for ks in at for part in ks]

    def rows(pieces, begun, last):
        return hessian_rows(place, apart, dp_size, pieces, tokens, owned, begun, last)

    begun = rows(near[:1], None, False)
    begun = rows(near[1:], begun, not far)
    begun, columns, *far = lax.optimization_barrier((begun, columns, *far))
    examples = tokens // LEN
    devices = owners * pipe_size
    shares = solve(
        place, apart, near + far, where, columns, tokens, examples, parts, devices
    )
    shares = lax.all_to_all(shares, ("tensor", "dp", "pipe"), 0, 0, tiled=True)
    scores = jnp.sum(shares, axis=0)
    if far:
        begun = rows(far, begun, True)
    return (begun[None], scores)


def solution(mesh):
    in_specs = (
        P(("groups", "dp"), "tensor"),
        P("pipe", ("groups", "dp"), "tensor"),
        P("pipe", "tensor", None),
        P("pipe", "tensor", None),
        P("pipe", ("tensor", "dp"), None),
    )
    out_specs = (P("pipe", ("groups", "tensor", "dp"), None), P("groups", None))
    return jax.shard_map(shards, mesh=mesh, in_specs=in_specs, out_specs=out_specs, check_vma=False)
```

```python
import functools

import jax
import jax.numpy as jnp
from jax import lax
from jax.experimental import pallas as pl
from jax.experimental.pallas import tpu as pltpu
from jax.sharding import PartitionSpec as P

LEN = 1024
ITERS = 6
DAMPING = 0.1
NT = (((1,), (1,)), ((), ()))
VMEM_BYTES = 56 * 1024 * 1024


def whole_spec(shape):
    zeros = (0,) * len(shape)
    return pl.BlockSpec(shape, lambda *_: zeros)


def swap(value, axes, size, offset):
    return lax.ppermute(value, axes, [(i, i ^ offset) for i in range(size)])


def encode(value):
    return (value * jnp.abs(value)).astype(jnp.bfloat16)


def decode(code):
    wide = code.astype(jnp.float32)
    root = jnp.sqrt(jnp.abs(wide))
    return jnp.where(wide < 0, -root, root)


def order(position, count, first):
    bits = (count - 1).bit_length()
    offset = first
    for b in range(bits):
        bit = lax.shift_right_logical(position, jnp.int32(bits - 1 - b)) & 1
        offset = offset + bit * (2 << b)
    return offset


def project_kernel(sent, place, inputs, grads, proj_in, proj_out, out):
    x = lax.dot_general(proj_in[...], inputs[...], NT, preferred_element_type=jnp.float32)
    g = lax.dot_general(proj_out[...], grads[...], NT, preferred_element_type=jnp.float32)
    rank = x.shape[0]
    out[0, :rank, :] = encode(x) if sent else x
    out[0, rank:, :] = encode(g) if sent else g


def project(place, inputs, grads, proj_in, proj_out, parts, sent):
    rank, features = proj_in.shape
    hidden = proj_out.shape[1]
    block = inputs.shape[0] // parts
    tile = min(block, 256)
    split = block // tile
    count = parts // 2

    def rows(step, place):
        part = lax.bitwise_xor(place[0], order(step // split, count, 1 if sent else 0))
        return (part * split + lax.rem(step, split), 0)

    return pl.pallas_call(
        functools.partial(project_kernel, sent),
        grid_spec=pltpu.PrefetchScalarGridSpec(
            num_scalar_prefetch=1,
            grid=(count * split,),
            in_specs=[
                pl.BlockSpec((tile, features), rows),
                pl.BlockSpec((tile, hidden), rows),
                whole_spec(proj_in.shape),
                whole_spec(proj_out.shape),
            ],
            out_specs=pl.BlockSpec(
                (1, 2 * rank, tile), lambda step, place: (step // split, 0, lax.rem(step, split))
            ),
        ),
        out_shape=jax.ShapeDtypeStruct(
            (count, 2 * rank, block), jnp.bfloat16 if sent else jnp.float32
        ),
        compiler_params=pltpu.CompilerParams(vmem_limit_bytes=VMEM_BYTES),
        cost_estimate=pl.CostEstimate(
            flops=2 * count * block * (features + hidden) * rank,
            bytes_accessed=2 * count * block * (features + hidden),
            transcendentals=0,
        ),
        name="project_sent" if sent else "project_kept",
    )(place, inputs, grads, proj_in, proj_out)


def split_queries_kernel(queries, out):
    owners, rank, width = out.shape
    cols = queries.shape[1] // owners
    for i in range(width // cols):
        rows = queries[i * rank : (i + 1) * rank, :]
        for k in range(owners):
            out[k, :, i * cols : (i + 1) * cols] = rows[:, k * cols : (k + 1) * cols]


def split_queries(queries, owners, rank):
    rows, total = queries.shape
    shape = (owners, rank, (rows // rank) * (total // owners))
    return pl.pallas_call(
        split_queries_kernel,
        out_shape=jax.ShapeDtypeStruct(shape, jnp.float32),
        compiler_params=pltpu.CompilerParams(vmem_limit_bytes=VMEM_BYTES),
        name="split_queries",
    )(queries)


def solve_kernel(tokens, count, parts_at, place, apart, *refs):
    pieces = refs[:count]
    queries, scores, kept, x_s, g_s, pair, direction, residual, image, sums, w_even, w_odd = refs[
        count:
    ]
    side, cols, rank = direction.shape
    chunks, _, wide = x_s.shape
    each, _, block = pieces[0].shape
    owners, _, width = queries.shape
    mine = side // owners
    real = width // mine
    for c in range(chunks):
        n, at = divmod(c * wide, block)
        piece = pieces[n // each]
        x_s[c] = piece[n % each, :rank, at : at + wide].astype(jnp.float32)
        g = piece[n % each, rank:, at : at + wide]
        g_s[c, :rank, :] = g
        g_s[c, rank:, :] = g
    if real < cols:
        direction[...] = jnp.zeros_like(direction)
    for k in range(owners):
        turned = queries[k].T
        for i in range(mine):
            direction[k * mine + i, :real, :] = turned[i * real : (i + 1) * real, :]
    residual[...] = direction[...]
    bank = (w_even, w_odd)

    def total(value):
        return jnp.sum(jnp.sum(value, axis=0), axis=1, keepdims=True)

    def expand(c):
        bank[c % 2][...] = jnp.dot(pair[...], g_s[c], preferred_element_type=jnp.float32)

    def collect(c):
        u = jnp.zeros((cols, wide), jnp.float32)
        for i in range(side):
            u = u + bank[c % 2][i * cols : (i + 1) * cols, :] * x_s[c, i : i + 1, :]
        return u

    def spread(c, u):
        terms = [(u * x_s[c, i : i + 1, :]).astype(jnp.bfloat16) for i in range(side)]
        part = lax.dot_general(
            jnp.concatenate(terms, axis=0),
            g_s[c, :rank, :],
            NT,
            preferred_element_type=jnp.float32,
        ).reshape(side, cols, rank)
        image[...] = part if c == 0 else image[...] + part

    def fold(value):
        return functools.reduce(jnp.add, [value[:, k : k + 128] for k in range(0, wide, 128)])

    def apply(back):
        d = direction[...]
        high = d.astype(jnp.bfloat16)
        low = (d - high.astype(jnp.float32)).astype(jnp.bfloat16)
        pair[...] = jnp.concatenate([high, low], axis=2).reshape(side * cols, 2 * rank)
        energy = jnp.zeros((cols, 128), jnp.float32)
        expand(0)
        for c in range(chunks):
            if c + 1 < chunks:
                expand(c + 1)
            u = collect(c)
            if back:
                spread(c, u)
            sums[c] = fold(u)
            energy = energy + fold(u * u)
        return total(d * d), jnp.sum(energy, axis=1, keepdims=True)

    def advance(norm, length, energy):
        alpha = norm / (energy * (1.0 / tokens) + DAMPING * length)
        for c in range(chunks):
            kept[c] += alpha * sums[c]
        return alpha

    kept[...] = jnp.zeros_like(kept)

    def one_step(_, norm):
        alpha = advance(norm, *apply(True))
        d = direction[...]
        r = residual[...] - alpha * (image[...] * (1.0 / tokens) + DAMPING * d)
        residual[...] = r
        later = total(r * r)
        direction[...] = r + later / norm * d
        return later

    norm = lax.fori_loop(0, ITERS - 1, one_step, total(residual[...] * residual[...]))
    advance(norm, *apply(False))

    scores[...] = jnp.zeros_like(scores)
    lane = lax.broadcasted_iota(jnp.int32, (cols, 128), 1)
    column = lax.broadcasted_iota(jnp.int32, (cols, 128), 0)
    owner = place[0] * (owners // parts_at[1]) + apart[0]
    here = (lane == column + owner * real) & (column < real)
    for c in range(chunks):
        n, at = divmod(c * wide, block)
        away, k = parts_at[0][n]
        example = lax.bitwise_xor(apart[0], away) * parts_at[2] + lax.div(
            lax.bitwise_xor(place[0], k) * block + at, LEN
        )
        value = jnp.sum(kept[c], axis=1, keepdims=True) * (1.0 / LEN)
        row = jnp.sum(jnp.where(here, value, 0.0), axis=0, keepdims=True)
        scores[0, pl.ds(example, 1), :] += row
    for k in range(1, scores.shape[0]):
        scores[k] = scores[0]


def solve(place, apart, pieces, where, queries, tokens, examples, parts, devices):
    owners, rank, width = queries.shape
    cols = max(owners * width // rank, 16)
    count, block = len(pieces), pieces[0].shape[2]
    wide = min(512, block)
    chunks = tokens // wide
    vectors = pltpu.VMEM((rank, cols, rank), jnp.float32)
    sums = pltpu.VMEM((chunks, cols, 128), jnp.float32)
    product = pltpu.VMEM((rank * cols, wide), jnp.float32)
    smem = pl.BlockSpec(memory_space=pltpu.SMEM)
    dp_size = owners // parts
    return pl.pallas_call(
        functools.partial(solve_kernel, tokens, count, (where, parts, examples // dp_size)),
        in_specs=[smem, smem] + [pl.BlockSpec(memory_space=pltpu.VMEM)] * (count + 1),
        out_specs=pl.BlockSpec(memory_space=pltpu.VMEM),
        out_shape=jax.ShapeDtypeStruct((devices, examples, 128), jnp.float32),
        scratch_shapes=[
            sums,
            pltpu.VMEM((chunks, rank, wide), jnp.float32),
            pltpu.VMEM((chunks, 2 * rank, wide), jnp.bfloat16),
            pltpu.VMEM((rank * cols, 2 * rank), jnp.bfloat16),
            vectors,
            vectors,
            vectors,
            sums,
            product,
            product,
        ],
        compiler_params=pltpu.CompilerParams(vmem_limit_bytes=VMEM_BYTES),
        cost_estimate=pl.CostEstimate(
            flops=2 * 2 * ITERS * 4 * tokens * cols * rank * rank,
            bytes_accessed=4 * tokens * rank,
            transcendentals=0,
        ),
        name="solve",
    )(place, apart, *pieces, queries)


def hessian_kernel(tokens, count, dp_size, first, last, place, apart, *refs):
    pieces = refs[:count]
    before = None if first else refs[count]
    out, x_s, g_s, own, even, odd = refs[-6:]
    step = pl.program_id(0)
    steps = pl.num_programs(0)
    rank = x_s.shape[0]
    each, _, block = pieces[0].shape
    rows = out.shape[0]
    columns = even.shape[0]
    first_row = (place[0] * dp_size + apart[0]) * rows

    def vectors(i):
        return x_s[pl.ds(i, 1), :].astype(jnp.bfloat16) * g_s[...]

    def form(target, tile):
        for j in range(columns // rank):
            target[j * rank : (j + 1) * rank, :] = vectors(tile * (columns // rank) + j)

    def product(source, half):
        at = slice(half * columns, (half + 1) * columns)
        gram = lax.dot_general(own[...], source[...], NT, preferred_element_type=jnp.float32)
        if not first:
            gram = gram + before[:, at]
        if last:
            shape = (rows, columns)
            row = lax.broadcasted_iota(jnp.int32, shape, 0) + first_row
            column = lax.broadcasted_iota(jnp.int32, shape, 1) + (2 * step + half) * columns
            gram = gram * (1.0 / tokens) + jnp.where(row == column, DAMPING, 0.0)
        out[:, at] = gram

    @pl.when(step == 0)
    def _():
        for n in range(count * each):
            at = slice(n * block, (n + 1) * block)
            x_s[:, at] = pieces[n // each][n % each, :rank, :].astype(jnp.float32)
            g_s[:, at] = pieces[n // each][n % each, rank:, :]
        for i in range(rows // rank):
            own[i * rank : (i + 1) * rank, :] = vectors(first_row // rank + i)
        form(even, 0)

    form(odd, 2 * step + 1)
    product(even, 0)
    form(even, lax.rem(2 * step + 2, 2 * steps))
    product(odd, 1)


def hessian_rows(place, apart, dp_size, pieces, tokens, rows, before, last):
    rank = pieces[0].shape[1] // 2
    count = len(pieces)
    width = rank * rank
    columns = 512
    here = count * pieces[0].shape[0] * pieces[0].shape[2]
    first = before is None
    tile = pl.BlockSpec((rows, 2 * columns), lambda step: (0, step))
    return pl.pallas_call(
        functools.partial(hessian_kernel, tokens, count, dp_size, first, last),
        grid=(width // (2 * columns),),
        in_specs=[pl.BlockSpec(memory_space=pltpu.SMEM)] * 2
        + [whole_spec(pieces[0].shape)] * count
        + ([] if first else [tile]),
        out_specs=tile,
        out_shape=jax.ShapeDtypeStruct((rows, width), jnp.float32),
        scratch_shapes=[
            pltpu.VMEM((rank, here), jnp.float32),
            pltpu.VMEM((rank, here), jnp.bfloat16),
            pltpu.VMEM((rows, here), jnp.bfloat16),
            pltpu.VMEM((columns, here), jnp.bfloat16),
            pltpu.VMEM((columns, here), jnp.bfloat16),
        ],
        input_output_aliases={} if first else {2 + count: 0},
        compiler_params=pltpu.CompilerParams(vmem_limit_bytes=VMEM_BYTES),
        cost_estimate=pl.CostEstimate(
            flops=2 * rows * width * here,
            bytes_accessed=(1 if first else 2) * 4 * rows * width,
            transcendentals=0,
        ),
        name="hessian_first" if first else "hessian_rest",
    )(place, apart, *pieces, *([] if first else [before]))


def shards(layer_input, out_grads, proj_in, proj_out, queries):
    rank = proj_in.shape[2]
    parts, dp_size, pipe_size = (lax.axis_size(a) for a in ("tensor", "dp", "pipe"))
    owners = parts * dp_size
    tok_dev = layer_input.shape[0]
    owned = queries.shape[1]
    place = lax.axis_index("tensor").astype(jnp.int32).reshape(1)
    apart = lax.axis_index("dp").astype(jnp.int32).reshape(1)
    tokens = tok_dev * dp_size

    operands = (place, layer_input, out_grads[0], proj_in[0].T, proj_out[0].T, parts)
    sent = swap(project(*operands, True), "tensor", parts, 1)
    total = project(*operands, False) + decode(sent)
    rows, total = lax.optimization_barrier((queries[0], total))
    cut = split_queries(rows, owners, rank)
    offset = 2
    while 2 * offset < parts:
        half = total.shape[0] // 2
        total = total[:half] + decode(swap(encode(total[half:]), "tensor", parts, offset))
        offset *= 2
    other = decode(swap(encode(total), "tensor", parts, offset))
    near = [jnp.stack([total[0] + other[1], total[1] + other[0]]).astype(jnp.bfloat16)]
    at = [[0, offset]]
    cut, near[0] = lax.optimization_barrier((cut, near[0]))
    columns = lax.all_to_all(cut, ("tensor", "dp"), 0, 0, tiled=True)

    while offset > 1:
        offset //= 2
        if offset < parts // 2:
            near = near + [swap(piece, "tensor", parts, offset) for piece in near]
            at = at + [[k ^ offset for k in ks] for ks in at]
    far = [swap(piece, "dp", dp_size, k) for k in range(1, dp_size) for piece in near]
    where = [(k, part) for k in range(dp_size) for ks in at for part in ks]

    begun = hessian_rows(place, apart, dp_size, near, tokens, owned, None, not far)
    begun, columns, *far = lax.optimization_barrier((begun, columns, *far))
    examples = tokens // LEN
    devices = owners * pipe_size
    shares = solve(
        place, apart, near + far, where, columns, tokens, examples, parts, devices
    )
    shares = lax.all_to_all(shares, ("tensor", "dp", "pipe"), 0, 0, tiled=True)
    scores = jnp.sum(shares, axis=0)
    if far:
        begun = hessian_rows(place, apart, dp_size, far, tokens, owned, begun, True)
    return (begun[None], scores)


def solution(mesh):
    in_specs = (
        P(("groups", "dp"), "tensor"),
        P("pipe", ("groups", "dp"), "tensor"),
        P("pipe", "tensor", None),
        P("pipe", "tensor", None),
        P("pipe", ("tensor", "dp"), None),
    )
    out_specs = (P("pipe", ("groups", "tensor", "dp"), None), P("groups", None))
    return jax.shard_map(shards, mesh=mesh, in_specs=in_specs, out_specs=out_specs, check_vma=False)
```
